512 devices in a mesh: dp: 8 (over y, core), row: 16 (over z_hi, x), col: 4 (over z_lo).
Axes of the slice: x: 4, y: 4, z: 16 (z_hi: 4, z_lo: 4; z = z_hi * 4 + z_lo), core: 2. Of those that a mesh axis runs over, the one named last changes fastest.
Arguments:
- activations: bfloat16 [8192, 4096], P(('dp', 'col'), 'row'), parts along dimension 0, may hold values from -6 to 6
- weight_codes: bfloat16 [4096, 14336], P('col', 'row'), may hold values from -3.75 to 3.75, as said below
- block_scales: bfloat16 [32, 112], P('col', 'row'), may hold values from 0.0039978027 to 0.039794922
- out_grad: bfloat16 [8192, 14336], P(('dp', 'col'), 'row'), parts along dimension 0, may hold values from -6 to 6
Outputs:
- projected: bfloat16 [8192, 14336], P(('dp', 'col'), 'row'), parts along dimension 0
- input_grad: bfloat16 [8192, 4096], P(('dp', 'col'), 'row'), parts along dimension 0
The draws below stay inside these ranges and needn't reach their ends.
There are 8 independent parts, one for each index of `dp`. The reference program is written for one: setup_inputs(seed, part) draws one part's arguments, and reference() takes and returns one part's arrays. A program takes and returns all parts, laid end to end along the dimension named above; an argument that names none is the same for every part. Nothing has to cross between parts.
Inputs may be any that keep to these rules, and one draw needn't show every extreme that they name: `weight_codes`: every entry is an FP8 e4m3 value, plus or minus (1 + m / 8) 2^e with m in 0 to 7 and e in -2 to 1.
All inputs are finite; a program needn't handle non-finite values.
Results may differ from the reference program's by a relative error of at most 0.02.
Values may be sent and summed in bfloat16 or wider, within the bound.
A program may use at most 64 MiB of HBM per device.

```python
import math
import jax
import jax.numpy as jnp
from jax import lax

D = 4096
FF = 14336
QB = 128
TOKENS = 1024
SD = 32
SF = 112
N_ROW = 16
N_COL = 4


def draw_weight_codes(key, part):
    key = jax.random.fold_in(key, 11)
    key_mant, key_expo, key_sign = jax.random.split(key, 3)
    mantissa = jax.random.randint(key_mant, (D, FF), 0, 8)
    exponent = jax.random.randint(key_expo, (D, FF), -2, 2)
    signs = jax.random.randint(key_sign, (D, FF), 0, 2)
    magnitude = (1.0 + mantissa.astype(jnp.float32) / 8.0) * jnp.exp2(exponent.astype(jnp.float32))
    values = magnitude * (2.0 * signs.astype(jnp.float32) - 1.0)
    return values.astype(jnp.bfloat16)


def level_of(key, shape, cuts, smallest, high):
    loudness, own = 1.0, jax.random.fold_in(key, 6)
    for position, shards_of in cuts:
        steps = jnp.exp(jax.random.uniform(jax.random.fold_in(own, position), (shards_of,), jnp.float32, smallest / len(cuts), high / len(cuts)))
        loudness = loudness * jnp.repeat(steps, shape[position] // shards_of).reshape([-1 if axis == position else 1 for axis in range(len(shape))])
    return loudness


def centred(stream_key, dims, width, reach, shards=(), held_as=jnp.bfloat16):
    level = level_of(stream_key, dims, shards, -0.22, 0.18) if shards else 1.0
    result = jax.random.normal(stream_key, dims, jnp.float32) * width * level
    return jnp.minimum(jnp.maximum(result, -reach), reach).astype(held_as)


def setup_inputs(seed: int = 0, part: int = 0) -> dict:
    arg_keys = jax.random.split(jax.random.key(seed), 5)
    part_keys = jax.random.split(jax.random.fold_in(arg_keys[4], part), 5)
    return {
        "activations": centred(part_keys[0], (TOKENS, D), 1.0, 6.0, ((0, 4), (1, 16))),
        "weight_codes": draw_weight_codes(jax.random.fold_in(arg_keys[4], 71), part),
        "block_scales": jnp.clip(jnp.exp(math.log(0.039794922) - 2.2979944 * jax.random.uniform(arg_keys[2], (SD, SF), jnp.float32) ** level_of(arg_keys[2], (SD, SF), ((0, 4), (1, 16)), -0.2, 0.2)), 0.0039978027, 0.039794922).astype(jnp.bfloat16),
        "out_grad": centred(part_keys[3], (TOKENS, FF), 1.0, 6.0, ((0, 4), (1, 16))),
    }


def dequantize(weight_codes, block_scales):
    height, breadth = weight_codes.shape
    blocks = weight_codes.astype(jnp.float32).reshape(height // QB, QB, breadth // QB, QB)
    scaled = blocks * block_scales.astype(jnp.float32)[:, None, :, None]
    return scaled.reshape(height, breadth).astype(jnp.bfloat16)


def reference(activations, weight_codes, block_scales, out_grad):
    weight = dequantize(weight_codes, block_scales)
    col_width = D // N_COL
    projected = jnp.zeros((TOKENS, FF), jnp.float32)
    for column in range(N_COL):
        first_col = column * col_width
        product = jnp.dot(activations[:, first_col:first_col + col_width], weight[first_col:first_col + col_width], preferred_element_type=jnp.float32)
        projected = projected + lax.optimization_barrier(product.astype(jnp.bfloat16)).astype(jnp.float32)
    row_width = FF // N_ROW
    gradient = jnp.zeros((TOKENS, D), jnp.float32)
    for row_index in range(N_ROW):
        first_unit = row_index * row_width
        product = lax.dot_general(out_grad[:, first_unit:first_unit + row_width], weight[:, first_unit:first_unit + row_width], (((1,), (1,)), ((), ())), preferred_element_type=jnp.float32)
        gradient = gradient + lax.optimization_barrier(product.astype(jnp.bfloat16)).astype(jnp.float32)
    return projected.astype(jnp.bfloat16), gradient.astype(jnp.bfloat16)
```

```python
import jax
import jax.numpy as jnp
from jax import lax
from jax.experimental import pallas as pl
from jax.experimental.pallas import tpu as pltpu
from jax.sharding import PartitionSpec as P

QB = 128
F32 = jnp.float32
BF16 = jnp.bfloat16
MESH = pl.DeviceIdType.MESH


def kernel(
    act_hbm, codes_hbm, scales_ref, grad_hbm, proj_ref, igrad_ref,
    codes, grad, weight, acts, total,
    part_out, part_in_half, part_in, sums, far_out, far_in_half, far_in,
    local_sem,
    wz_send, wz_recv, wy_send, wy_recv, wc_send, wc_recv,
    az_send, az_recv, ax_send, ax_recv,
    gx_send, gx_recv, gz_send, gz_recv,
):
    dp, row, zl = lax.axis_index("dp"), lax.axis_index("row"), lax.axis_index("col")
    y, c = dp // 2, dp % 2
    zh, x = row // 4, row % 4

    def at(dy=0, dc=0, dz=0, dx=0):
        return (((y + dy) % 4) * 2 + (c + dc) % 2, ((zh + dz) % 4) * 4 + (x + dx) % 4, zl)

    LEFT, RIGHT = -1, 1
    x_at = {d: at(dx=d) for d in (LEFT, RIGHT)}
    y_at = {d: at(dy=d) for d in (LEFT, RIGHT)}
    z_at = {d: at(dz=d) for d in (LEFT, RIGHT)}
    other_core = at(dc=1)

    def line_at(col):
        return (dp, row, col)

    s_of = [
        zl,
        jnp.where(zl % 2 == 0, zl + 1, zl - 1),
        jnp.where(zl < 2, 2, 1),
        jnp.where(zl < 2, 3, 0),
    ]

    copies = []

    def remote(src, dst, ssem, rsem, dev):
        return pltpu.make_async_remote_copy(
            src_ref=src, dst_ref=dst, send_sem=ssem, recv_sem=rsem, device_id=dev, device_id_type=MESH
        )

    def send(src, dst, ssem, rsem, dev):
        copy = remote(src, dst, ssem, rsem, dev)
        copy.start()
        copies.append(copy)

    def arrived(dst, ssem, rsem):
        remote(dst, dst, ssem, rsem, other_core).wait_recv()

    load_codes = pltpu.make_async_copy(codes_hbm, codes, local_sem.at[0])
    load_act = pltpu.make_async_copy(act_hbm, acts.at[row], local_sem.at[1])
    load_grad = pltpu.make_async_copy(grad_hbm, grad, local_sem.at[2])
    load_codes.start()
    load_act.start()
    load_grad.start()

    barrier = pltpu.get_barrier_semaphore()
    for dev in (*x_at.values(), *y_at.values(), *z_at.values(), other_core):
        pl.semaphore_signal(barrier, inc=1, device_id=dev, device_id_type=MESH)

    @pl.when(zl > 0)
    def _():
        pl.semaphore_signal(barrier, inc=1, device_id=line_at(zl - 1), device_id_type=MESH)

    @pl.when(zl < 3)
    def _():
        pl.semaphore_signal(barrier, inc=1, device_id=line_at(zl + 1), device_id_type=MESH)

    def half(core):
        return pl.ds(pl.multiple_of(core * QB, QB), QB)

    mine = half(c)
    theirs = half(1 - c)
    scales = scales_ref[...].astype(F32)
    scale_row = lax.broadcasted_iota(jnp.int32, scales.shape, 0)

    def dequantize(j):
        scale = jnp.sum(jnp.where(scale_row == j, scales, 0.0), axis=0, keepdims=True)
        rows = pl.ds(pl.multiple_of(j * QB, QB), QB)
        place = zl * 4 + j // 2
        for b in range(codes.shape[1] // QB):
            cols = pl.ds(b * QB, QB)
            value = codes[rows, cols].astype(F32) * scale[:, b:b + 1]
            weight[place, half(j % 2), cols] = value.astype(BF16)

    load_codes.wait()
    dequantize(dp)
    load_act.wait()
    pl.semaphore_wait(barrier, 7 + jnp.where(zl > 0, 1, 0) + jnp.where(zl < 3, 1, 0))

    own_slice = weight.at[zl * 4 + y, mine]

    def line_copy(s, target, slot):
        w = weight.at[s * 4 + y, mine]
        return remote(w, w, wz_send.at[slot], wz_recv.at[s], line_at(target))

    @pl.when(zl < 3)
    def _():
        line_copy(zl, zl + 1, 0).start()

    @pl.when(zl > 0)
    def _():
        line_copy(zl, zl - 1, 1).start()

    first, second = pl.ds(0, 128), pl.ds(128, 128)

    def acts_z_own():
        a = acts.at[row]
        for i, d in enumerate((LEFT, RIGHT)):
            send(a, a, az_send.at[i], az_recv.at[i], z_at[d])

    def acts_z_relay():
        for i, (d, rows) in enumerate(((LEFT, second), (RIGHT, first))):
            block = acts.at[((zh - d) % 4) * 4 + x]
            arrived(block, az_send.at[i], az_recv.at[i])
            piece = block.at[rows]
            send(piece, piece, az_send.at[2 + i], az_recv.at[2 + i], z_at[d])

    def acts_z_far():
        block = acts.at[((zh + 2) % 4) * 4 + x]
        for i, rows in enumerate((second, first)):
            arrived(block.at[rows], az_send.at[2 + i], az_recv.at[2 + i])

    def acts_x_own(k):
        b = (zh + k) % 4
        a = acts.at[b * 4 + x]
        for i, d in enumerate((LEFT, RIGHT)):
            send(a, a, ax_send.at[k, i], ax_recv.at[k, i], x_at[d])

    def acts_x_relay(k):
        b = (zh + k) % 4
        for i, (d, rows) in enumerate(((LEFT, second), (RIGHT, first))):
            block = acts.at[b * 4 + (x - d) % 4]
            arrived(block, ax_send.at[k, i], ax_recv.at[k, i])
            piece = block.at[rows]
            send(piece, piece, ax_send.at[k, 2 + i], ax_recv.at[k, 2 + i], x_at[d])

    def acts_x_far(k):
        block = acts.at[((zh + k) % 4) * 4 + (x + 2) % 4]
        for i, rows in enumerate((second, first)):
            arrived(block.at[rows], ax_send.at[k, 2 + i], ax_recv.at[k, 2 + i])

    def w_line(k):
        s = s_of[k]
        w = weight.at[s * 4 + y, mine]
        arrived(w, wz_send.at[0], wz_recv.at[s])
        onward = jnp.where(s > zl, zl - 1, zl + 1)

        @pl.when((onward >= 0) & (onward <= 3))
        def _():
            line_copy(s, onward, 1 + k).start()

        for i, d in enumerate((LEFT, RIGHT)):
            send(w, w, wy_send.at[k, i], wy_recv.at[k, i], y_at[d])
        send(w, w, wc_send.at[k, 0], wc_recv.at[k, 0], other_core)

    def rows_of(i):
        return pl.ds(pl.multiple_of(c * QB + i * (QB // 2), QB // 2), QB // 2)

    def w_y_relay(k):
        s = s_of[k]
        for i, (d, h) in enumerate(((LEFT, 1), (RIGHT, 0))):
            place = s * 4 + (y - d) % 4
            w = weight.at[place, mine]
            arrived(w, wy_send.at[k, i], wy_recv.at[k, i])
            piece = weight.at[place, rows_of(h)]
            send(piece, piece, wy_send.at[k, 2 + i], wy_recv.at[k, 2 + i], y_at[d])
            send(w, w, wc_send.at[k, 1 + i], wc_recv.at[k, 1 + i], other_core)

    def w_y_far(k):
        place = s_of[k] * 4 + (y + 2) % 4
        for i, h in enumerate((1, 0)):
            arrived(weight.at[place, rows_of(h)], wy_send.at[k, 2 + i], wy_recv.at[k, 2 + i])
        w = weight.at[place, mine]
        send(w, w, wc_send.at[k, 3], wc_recv.at[k, 3], other_core)

    def w_core(k):
        s = s_of[k]
        for i, dy in enumerate((0, -LEFT, -RIGHT, 2)):
            arrived(weight.at[s * 4 + (y + dy) % 4, theirs], wc_send.at[k, i], wc_recv.at[k, i])

    def partial(k, dx):
        w = weight[s_of[k] * 4 + (x + dx) % 4]
        return lax.dot_general(grad[...], w, (((1,), (1,)), ((), ())), preferred_element_type=F32)

    def g_x_half(k):
        part_out[k, 2] = partial(k, 2).astype(BF16)
        for i, (d, rows) in enumerate(((LEFT, second), (RIGHT, first))):
            send(part_out.at[k, 2, rows], part_in_half.at[k, i], gx_send.at[k, i], gx_recv.at[k, i], x_at[d])

    def g_x_full(k):
        for i, (d, rows) in enumerate(((LEFT, second), (RIGHT, first))):
            part = partial(k, d)
            arrived(part_in_half.at[k, i], gx_send.at[k, i], gx_recv.at[k, i])
            came = part_in_half[k, i].astype(F32)
            if i == 0:
                part_out[k, i, 0:128] = part[0:128].astype(BF16)
                part_out[k, i, 128:256] = (part[128:256] + came).astype(BF16)
            else:
                part_out[k, i, 0:128] = (part[0:128] + came).astype(BF16)
                part_out[k, i, 128:256] = part[128:256].astype(BF16)
            send(part_out.at[k, i], part_in.at[k, i], gx_send.at[k, 2 + i], gx_recv.at[k, 2 + i], x_at[d])

    def far_copy(i, rows, slot):
        d = (LEFT, RIGHT)[i]
        if slot < 2:
            return remote(far_out.at[2, rows], far_in_half.at[i], gz_send.at[slot], gz_recv.at[slot], z_at[d])
        return remote(far_out.at[i], far_in.at[i], gz_send.at[slot], gz_recv.at[slot], z_at[d])

    def g_x_sum(k):
        part = partial(k, 0)
        for i in range(2):
            arrived(part_in.at[k, i], gx_send.at[k, 2 + i], gx_recv.at[k, 2 + i])
            part += part_in[k, i].astype(F32)
        away = (s_of[k] - zh) % 4

        @pl.when(away == 2)
        def _():
            far_out[2] = part.astype(BF16)
            far_copy(0, second, 0).start()
            far_copy(1, first, 1).start()

        @pl.when(away != 2)
        def _():
            sums[away] = part

    def g_z_full(k):
        away = (s_of[k] - zh) % 4

        @pl.when(away == 3)
        def _():
            arrived(far_in_half.at[0], gz_send.at[0], gz_recv.at[0])
            far_out[0, 0:128] = sums[3, 0:128].astype(BF16)
            far_out[0, 128:256] = (sums[3, 128:256] + far_in_half[0].astype(F32)).astype(BF16)
            far_copy(0, None, 2).start()

        @pl.when(away == 1)
        def _():
            arrived(far_in_half.at[1], gz_send.at[1], gz_recv.at[1])
            far_out[1, 0:128] = (sums[1, 0:128] + far_in_half[1].astype(F32)).astype(BF16)
            far_out[1, 128:256] = sums[1, 128:256].astype(BF16)
            far_copy(1, None, 3).start()

    def g_z_sum():
        part = sums[0]
        for i in range(2):
            arrived(far_in.at[i], gz_send.at[2 + i], gz_recv.at[2 + i])
            part += far_in[i].astype(F32)
        igrad_ref[...] = part.astype(BF16)

    def forward(k, start=False):
        s = s_of[k]

        @pl.loop(0, 4)
        def _(i):
            block = s * 4 + i
            term = jnp.dot(acts[block], weight[block], preferred_element_type=F32)
            if start:
                @pl.when(i == 0)
                def _():
                    total[...] = term

                @pl.when(i > 0)
                def _():
                    total[...] += term
            else:
                total[...] += term

    acts_x_own(0)
    acts_z_own()

    @pl.loop(1, 8)
    def _(step):
        dequantize((dp + step) % 8)

    load_grad.wait()
    g_x_half(0)
    w_line(1)
    g_x_full(0)
    acts_x_relay(0)
    w_line(2)
    w_y_relay(1)
    g_x_sum(0)
    acts_z_relay()
    acts_x_own(1)
    acts_x_own(3)
    acts_x_far(0)
    w_line(3)
    w_y_far(1)
    w_core(1)
    g_x_half(1)
    w_y_relay(2)
    acts_x_relay(1)
    acts_x_relay(3)
    g_z_full(0)
    g_x_full(1)
    acts_z_far()
    acts_x_own(2)
    w_y_far(2)
    w_core(2)
    g_x_half(2)
    w_y_relay(3)
    g_x_sum(1)
    acts_x_far(1)
    acts_x_far(3)
    g_x_full(2)
    g_z_full(1)
    acts_x_relay(2)
    w_y_far(3)
    w_core(3)
    g_x_half(3)
    g_x_sum(2)
    acts_x_far(2)
    forward(0, True)
    g_x_full(3)
    g_z_full(2)
    forward(1)
    g_x_sum(3)
    forward(2)
    g_z_full(3)
    forward(3)
    proj_ref[...] = total[...].astype(BF16)
    g_z_sum()

    for copy in copies:
        copy.wait_send()

    @pl.when(zl < 3)
    def _():
        line_copy(zl, zl + 1, 0).wait_send()

    @pl.when(zl > 0)
    def _():
        line_copy(zl, zl - 1, 1).wait_send()

    for k in (1, 2, 3):
        onward = jnp.where(s_of[k] > zl, zl - 1, zl + 1)

        @pl.when((onward >= 0) & (onward <= 3))
        def _():
            line_copy(s_of[k], onward, 1 + k).wait_send()

    far_copy(0, second, 0).wait_send()
    far_copy(1, first, 1).wait_send()
    far_copy(0, None, 2).wait_send()
    far_copy(1, None, 3).wait_send()


def local(activations, weight_codes, block_scales, out_grad):
    tokens, features = activations.shape
    depth, units = weight_codes.shape
    any_ref = pl.BlockSpec(memory_space=pl.ANY)
    vmem_ref = pl.BlockSpec(memory_space=pltpu.VMEM)
    dma = pltpu.SemaphoreType.DMA
    square = (tokens, features)
    half_square = (tokens // 2, features)
    return pl.pallas_call(
        kernel,
        out_shape=(
            jax.ShapeDtypeStruct((tokens, units), BF16),
            jax.ShapeDtypeStruct((tokens, features), BF16),
        ),
        in_specs=[any_ref, any_ref, vmem_ref, any_ref],
        out_specs=(vmem_ref, vmem_ref),
        scratch_shapes=[
            pltpu.VMEM((depth, units), BF16),
            pltpu.VMEM((tokens, units), BF16),
            pltpu.VMEM((16, 2 * QB, units), BF16),
            pltpu.VMEM((16, *square), BF16),
            pltpu.VMEM((tokens, units), F32),
            pltpu.VMEM((4, 3, *square), BF16),
            pltpu.VMEM((4, 2, *half_square), BF16),
            pltpu.VMEM((4, 2, *square), BF16),
            pltpu.VMEM((4, *square), F32),
            pltpu.VMEM((3, *square), BF16),
            pltpu.VMEM((2, *half_square), BF16),
            pltpu.VMEM((2, *square), BF16),
            dma((3,)),
            dma((5,)), dma((4,)),
            dma((4, 4)), dma((4, 4)),
            dma((4, 4)), dma((4, 4)),
            dma((4,)), dma((4,)),
            dma((4, 4)), dma((4, 4)),
            dma((4, 4)), dma((4, 4)),
            dma((4,)), dma((4,)),
        ],
        compiler_params=pltpu.CompilerParams(
            collective_id=0, has_side_effects=True, vmem_limit_bytes=48 * 2**20
        ),
        cost_estimate=pl.CostEstimate(
            flops=4 * tokens * 16 * features * units, bytes_accessed=4 * depth * units, transcendentals=0
        ),
        name="up_projection",
    )(activations, weight_codes, block_scales, out_grad)


def solution(mesh):
    return jax.shard_map(
        local,
        mesh=mesh,
        in_specs=(
            P(("dp", "col"), "row"),
            P("col", "row"),
            P("col", "row"),
            P(("dp", "col"), "row"),
        ),
        out_specs=(P(("dp", "col"), "row"), P(("dp", "col"), "row")),
        check_vma=False,
    )
```

```python
import jax
import jax.numpy as jnp
from jax import lax
from jax.experimental import pallas as pl
from jax.experimental.pallas import tpu as pltpu
from jax.sharding import PartitionSpec as P

QB = 128
F32 = jnp.float32
BF16 = jnp.bfloat16
MESH = pl.DeviceIdType.MESH


def kernel(
    act_hbm, codes_hbm, scales_ref, grad_hbm, proj_ref, igrad_ref,
    codes, grad, weight, acts, total,
    part, part_out, part_in_half, part_in, sums, far_out, far_in_half, far_in,
    proj_out, proj_in, igrad_out, igrad_in,
    local_sem, swap_send, swap_recv,
    wz_send, wz_recv, wy_send, wy_recv,
    az_send, az_recv, ax_send, ax_recv,
    gx_send, gx_recv, gz_send, gz_recv,
):
    dp, row, zl = lax.axis_index("dp"), lax.axis_index("row"), lax.axis_index("col")
    y, c = dp // 2, dp % 2
    zh, x = row // 4, row % 4

    def at(dy=0, dc=0, dz=0, dx=0):
        return (((y + dy) % 4) * 2 + (c + dc) % 2, ((zh + dz) % 4) * 4 + (x + dx) % 4, zl)

    LEFT, RIGHT = -1, 1
    x_at = {d: at(dx=d) for d in (LEFT, RIGHT)}
    y_at = {d: at(dy=d) for d in (LEFT, RIGHT)}
    z_at = {d: at(dz=d) for d in (LEFT, RIGHT)}
    other_core = at(dc=1)

    def line_at(col):
        return (dp, row, col)

    s_of = [zl, zl + 1 - 2 * (zl % 2), (zl + 2) % 4, 3 - zl]
    inside = (zl == 1) | (zl == 2)

    copies = []

    def remote(src, dst, ssem, rsem, dev):
        return pltpu.make_async_remote_copy(
            src_ref=src, dst_ref=dst, send_sem=ssem, recv_sem=rsem, device_id=dev, device_id_type=MESH
        )

    def send(src, dst, ssem, rsem, dev):
        copy = remote(src, dst, ssem, rsem, dev)
        copy.start()
        copies.append(copy)

    def arrived(dst, ssem, rsem):
        remote(dst, dst, ssem, rsem, other_core).wait_recv()

    def tile(i, size):
        return pl.ds(pl.multiple_of(i * size, size), size)

    def half_slice(s, dy, h):
        return weight.at[s, tile((y + dy) % 4 * 2 + h, QB // 2)]

    my_tokens, their_tokens = tile(c, 256), tile(1 - c, 256)

    load_codes = [
        pltpu.make_async_copy(codes_hbm.at[tile((y + i) % 4 * 2 + c, QB)], codes.at[i], local_sem.at[i]) for i in range(4)
    ]
    load_act = pltpu.make_async_copy(
        act_hbm.at[:, tile(c, QB)], acts.at[row, my_tokens], local_sem.at[4]
    )
    load_grad = pltpu.make_async_copy(grad_hbm, grad.at[my_tokens], local_sem.at[5])
    for load in (load_codes[0], load_act, load_grad, *load_codes[1:]):
        load.start()

    barrier = pltpu.get_barrier_semaphore()
    for dev in (*x_at.values(), *y_at.values(), *z_at.values(), other_core):
        pl.semaphore_signal(barrier, inc=1, device_id=dev, device_id_type=MESH)

    @pl.when(zl > 0)
    def _():
        pl.semaphore_signal(barrier, inc=1, device_id=line_at(zl - 1), device_id_type=MESH)

    @pl.when(zl < 3)
    def _():
        pl.semaphore_signal(barrier, inc=1, device_id=line_at(zl + 1), device_id_type=MESH)

    scales = scales_ref[...].astype(F32)
    scale_row = lax.broadcasted_iota(jnp.int32, scales.shape, 0)

    def dequantize(i):
        block = (y + i) % 4
        scale = jnp.sum(jnp.where(scale_row == block * 2 + c, scales, 0.0), axis=0, keepdims=True).astype(BF16)
        load_codes[i].wait()
        for b in range(codes.shape[2] // QB):
            cols = pl.ds(b * QB, QB)
            weight[zl, tile(block, QB), cols] = codes[i, :, cols] * scale[:, b:b + 1]

    dequantize(0)
    pl.semaphore_wait(barrier, 7 + jnp.where(zl > 0, 1, 0) + jnp.where(zl < 3, 1, 0))

    their_act = act_hbm.at[:, tile(1 - c, QB)]
    send(their_act, acts.at[row, my_tokens], swap_send.at[0], swap_recv.at[0], other_core)
    send(grad_hbm, grad.at[my_tokens], swap_send.at[1], swap_recv.at[1], other_core)

    def take_act():
        load_act.wait()
        arrived(acts.at[row, their_tokens], swap_send.at[0], swap_recv.at[0])

    def take_grad():
        load_grad.wait()
        arrived(grad.at[their_tokens], swap_send.at[1], swap_recv.at[1])

    def line_copy(s, target, slot, h):
        w = half_slice(s, 0, h)
        return remote(w, w, wz_send.at[slot, h], wz_recv.at[s, h], line_at(target))

    for h in (0, 1):
        @pl.when(zl < 3)
        def _():
            line_copy(zl, zl + 1, 0, h).start()

        @pl.when(zl > 0)
        def _():
            line_copy(zl, zl - 1, 1, h).start()

    first, second = pl.ds(0, 256), pl.ds(256, 256)

    ways = ((LEFT, second, first), (RIGHT, first, second))

    def acts_piece(b, block, rows):
        return acts.at[b * 4 + block, rows]

    def acts_z_own(rest):
        for i, (d, relayed, direct) in enumerate(ways):
            piece = acts_piece(zh, x, direct if rest else relayed)
            send(piece, piece, az_send.at[4 * rest + i], az_recv.at[4 * rest + i], z_at[d])

    def acts_z_relay():
        for i, (d, relayed, _) in enumerate(ways):
            piece = acts_piece((zh - d) % 4, x, relayed)
            arrived(piece, az_send.at[i], az_recv.at[i])
            send(piece, piece, az_send.at[2 + i], az_recv.at[2 + i], z_at[d])

    def acts_z_near():
        for i, (d, _, direct) in enumerate(ways):
            arrived(acts_piece((zh - d) % 4, x, direct), az_send.at[4 + i], az_recv.at[4 + i])

    def acts_z_far():
        for i, (_, relayed, _) in enumerate(ways):
            arrived(acts_piece((zh + 2) % 4, x, relayed), az_send.at[2 + i], az_recv.at[2 + i])

    def acts_x_own(k):
        for rest in (0, 1):
            for i, (d, relayed, direct) in enumerate(ways):
                piece = acts_piece((zh + k) % 4, x, direct if rest else relayed)
                send(piece, piece, ax_send.at[k, 4 * rest + i], ax_recv.at[k, 4 * rest + i], x_at[d])

    def acts_x_relay(k):
        for i, (d, relayed, _) in enumerate(ways):
            piece = acts_piece((zh + k) % 4, (x - d) % 4, relayed)
            arrived(piece, ax_send.at[k, i], ax_recv.at[k, i])
            send(piece, piece, ax_send.at[k, 2 + i], ax_recv.at[k, 2 + i], x_at[d])

    def acts_x_far(k):
        for i, (d, relayed, direct) in enumerate(ways):
            arrived(acts_piece((zh + k) % 4, (x - d) % 4, direct), ax_send.at[k, 4 + i], ax_recv.at[k, 4 + i])
            arrived(acts_piece((zh + k) % 4, (x + 2) % 4, relayed), ax_send.at[k, 2 + i], ax_recv.at[k, 2 + i])

    def w_take(k, h):
        s = s_of[k]
        arrived(half_slice(s, 0, h), wz_send.at[0, h], wz_recv.at[s, h])
        onward = jnp.where(s > zl, zl - 1, zl + 1)

        @pl.when((onward >= 0) & (onward <= 3))
        def _():
            line_copy(s, onward, 1 + k, h).start()

    def w_take_inside(h):
        @pl.when(inside)
        def _():
            w_take(3, h)

    def w_take_end(h):
        @pl.when(jnp.logical_not(inside))
        def _():
            w_take(3, h)

    def w_y_own(k, h):
        w = half_slice(s_of[k], 0, h)
        for i, d in enumerate((LEFT, RIGHT)):
            send(w, w, wy_send.at[k, i, h], wy_recv.at[k, i, h], y_at[d])

    def w_y_relay(k):
        for i, (d, h) in enumerate(((LEFT, 1), (RIGHT, 0))):
            w = half_slice(s_of[k], -d, h)
            arrived(w, wy_send.at[k, i, h], wy_recv.at[k, i, h])
            send(w, w, wy_send.at[k, 2 + i, h], wy_recv.at[k, 2 + i, h], y_at[d])

    def w_y_rest(k):
        for i, (d, h) in enumerate(((LEFT, 0), (RIGHT, 1))):
            arrived(half_slice(s_of[k], -d, h), wy_send.at[k, i, h], wy_recv.at[k, i, h])
        for i, h in enumerate((1, 0)):
            arrived(half_slice(s_of[k], 2, h), wy_send.at[k, 2 + i, h], wy_recv.at[k, 2 + i, h])

    def span(rows):
        return slice(rows.start, rows.start + rows.size)

    def share(k, dx, rows):
        return part[k, rows, tile((x + dx) % 4, QB)]

    def g_x_first(k):
        part[k] = lax.dot_general(grad[...], weight[s_of[k]], (((1,), (1,)), ((), ())), preferred_element_type=F32)
        part_out[k, 2] = share(k, 2, slice(None)).astype(BF16)
        for i, (d, relayed, _) in enumerate(ways):
            send(part_out.at[k, 2, relayed], part_in_half.at[k, i], gx_send.at[k, i], gx_recv.at[k, i], x_at[d])
        for i, (d, _, direct) in enumerate(ways):
            part_out[k, i, direct] = share(k, d, direct).astype(BF16)
            send(part_out.at[k, i, direct], part_in.at[k, i, direct], gx_send.at[k, 4 + i], gx_recv.at[k, 4 + i], x_at[d])

    def g_x_second(k):
        for i, (d, relayed, _) in enumerate(ways):
            arrived(part_in_half.at[k, i], gx_send.at[k, i], gx_recv.at[k, i])
            part_out[k, i, relayed] = (share(k, d, relayed) + part_in_half[k, i].astype(F32)).astype(BF16)
            send(part_out.at[k, i, relayed], part_in.at[k, i, relayed], gx_send.at[k, 2 + i], gx_recv.at[k, 2 + i], x_at[d])

    def far_copy(slot):
        i = slot % 2
        d, relayed, direct = ways[i]
        if slot < 2:
            src, dst = far_out.at[2, relayed], far_in_half.at[i]
        else:
            rows = relayed if slot < 4 else direct
            src, dst = far_out.at[i, rows], far_in.at[i, rows]
        return remote(src, dst, gz_send.at[slot], gz_recv.at[slot], z_at[d])

    def g_x_sum(k):
        own = share(k, 0, slice(None))
        for i, (_, relayed, direct) in enumerate(ways):
            arrived(part_in.at[k, i, direct], gx_send.at[k, 4 + i], gx_recv.at[k, 4 + i])
            arrived(part_in.at[k, i, relayed], gx_send.at[k, 2 + i], gx_recv.at[k, 2 + i])
            own += part_in[k, i].astype(F32)
        away = (s_of[k] - zh) % 4

        @pl.when(away == 2)
        def _():
            far_out[2] = own.astype(BF16)
            far_copy(0).start()
            far_copy(1).start()

        for i, (d, relayed, direct) in enumerate(ways):
            @pl.when(away == d % 4)
            def _():
                far_out[i, direct] = own[span(direct)].astype(BF16)
                far_copy(4 + i).start()
                sums[1 + i] = own

        @pl.when(away == 0)
        def _():
            sums[0] = own

    def g_z_second(k):
        away = (s_of[k] - zh) % 4
        for i, (d, relayed, _) in enumerate(ways):
            @pl.when(away == d % 4)
            def _():
                arrived(far_in_half.at[i], gz_send.at[i], gz_recv.at[i])
                far_out[i, relayed] = (sums[1 + i, relayed] + far_in_half[i].astype(F32)).astype(BF16)
                far_copy(2 + i).start()

    def g_z_sum():
        own = sums[0]
        for i, (_, relayed, direct) in enumerate(ways):
            arrived(far_in.at[i, direct], gz_send.at[4 + i], gz_recv.at[4 + i])
            arrived(far_in.at[i, relayed], gz_send.at[2 + i], gz_recv.at[2 + i])
            own += far_in[i].astype(F32)
        sums[0] = own
        igrad_out[...] = sums[0, their_tokens].astype(BF16)
        send(igrad_out, igrad_in, swap_send.at[2], swap_recv.at[2], other_core)
        igrad_ref[:, tile(c, QB)] = sums[0, my_tokens].astype(BF16)
        arrived(igrad_in, swap_send.at[2], swap_recv.at[2])
        igrad_ref[:, tile(1 - c, QB)] = igrad_in[...]

    def forward(k):
        s = s_of[k]
        rows = jnp.concatenate([acts[s * 4 + i] for i in range(4)], axis=1)
        term = jnp.dot(rows, weight[s], preferred_element_type=F32)
        if k == 0:
            total[...] = term
        else:
            total[...] += term

    def forward_swap():
        proj_out[...] = total[their_tokens].astype(BF16)
        send(proj_out, proj_in, swap_send.at[3], swap_recv.at[3], other_core)

    def forward_sum():
        arrived(proj_in, swap_send.at[3], swap_recv.at[3])
        proj_ref[...] = (total[my_tokens] + proj_in[...].astype(F32)).astype(BF16)

    dequantize(1)
    dequantize(3)
    w_take(1, 1)
    w_take_inside(1)
    w_y_own(1, 1)
    take_grad()
    dequantize(2)
    g_x_first(0)
    w_take_inside(0)
    w_take(1, 0)
    take_act()
    w_y_own(1, 0)
    w_take(2, 1)
    w_y_own(2, 1)
    w_take(2, 0)
    acts_x_own(0)
    w_y_own(2, 0)
    w_y_relay(1)
    w_take_end(0)
    acts_x_relay(0)
    acts_z_own(0)
    w_y_own(3, 0)
    w_take_end(1)
    w_y_own(3, 1)
    g_x_second(0)
    w_y_rest(1)
    w_y_relay(2)
    g_x_first(1)
    acts_z_own(1)
    w_y_relay(3)
    g_x_second(1)
    acts_z_relay()
    w_y_rest(2)
    acts_x_far(0)
    g_x_first(2)
    g_x_sum(1)
    w_y_rest(3)
    g_x_first(3)
    acts_z_near()
    g_x_second(2)
    g_x_second(3)
    g_x_sum(0)
    acts_x_own(3)
    g_x_sum(2)
    acts_x_own(1)
    acts_z_far()
    acts_x_own(2)
    g_x_sum(3)
    acts_x_relay(3)
    acts_x_relay(1)
    g_z_second(1)
    g_z_second(2)
    g_z_second(0)
    acts_x_relay(2)
    acts_x_far(3)
    g_z_second(3)
    acts_x_far(2)
    acts_x_far(1)
    forward(0)
    forward(1)
    forward(2)
    forward(3)
    forward_swap()
    g_z_sum()
    forward_sum()

    for copy in copies:
        copy.wait_send()

    for h in (0, 1):
        @pl.when(zl < 3)
        def _():
            line_copy(zl, zl + 1, 0, h).wait_send()

        @pl.when(zl > 0)
        def _():
            line_copy(zl, zl - 1, 1, h).wait_send()

    for k in (1, 2, 3):
        onward = jnp.where(s_of[k] > zl, zl - 1, zl + 1)
        for h in (0, 1):
            @pl.when((onward >= 0) & (onward <= 3))
            def _():
                line_copy(s_of[k], onward, 1 + k, h).wait_send()

    for slot in range(6):
        far_copy(slot).wait_send()


def local(activations, weight_codes, block_scales, out_grad):
    tokens, features = activations.shape
    depth, units = weight_codes.shape
    any_ref = pl.BlockSpec(memory_space=pl.ANY)
    vmem_ref = pl.BlockSpec(memory_space=pltpu.VMEM)
    dma = pltpu.SemaphoreType.DMA
    rows = depth // 2
    share = (2 * tokens, features // 2)
    half_share = (tokens, features // 2)
    return pl.pallas_call(
        kernel,
        out_shape=(
            jax.ShapeDtypeStruct((tokens, units), BF16),
            jax.ShapeDtypeStruct((tokens, features), BF16),
        ),
        in_specs=[any_ref, any_ref, vmem_ref, any_ref],
        out_specs=(vmem_ref, vmem_ref),
        scratch_shapes=[
            pltpu.VMEM((4, QB, units), BF16),
            pltpu.VMEM((2 * tokens, units), BF16),
            pltpu.VMEM((4, rows, units), BF16),
            pltpu.VMEM((16, 2 * tokens, QB), BF16),
            pltpu.VMEM((2 * tokens, units), F32),
            pltpu.VMEM((4, 2 * tokens, rows), F32),
            pltpu.VMEM((4, 3, *share), BF16),
            pltpu.VMEM((4, 2, *half_share), BF16),
            pltpu.VMEM((4, 2, *share), BF16),
            pltpu.VMEM((3, *share), F32),
            pltpu.VMEM((3, *share), BF16),
            pltpu.VMEM((2, *half_share), BF16),
            pltpu.VMEM((2, *share), BF16),
            pltpu.VMEM((tokens, units), BF16),
            pltpu.VMEM((tokens, units), BF16),
            pltpu.VMEM(half_share, BF16),
            pltpu.VMEM(half_share, BF16),
            dma((6,)), dma((4,)), dma((4,)),
            dma((5, 2)), dma((4, 2)),
            dma((4, 4, 2)), dma((4, 4, 2)),
            dma((6,)), dma((6,)),
            dma((4, 6)), dma((4, 6)),
            dma((4, 6)), dma((4, 6)),
            dma((6,)), dma((6,)),
        ],
        compiler_params=pltpu.CompilerParams(
            collective_id=0, has_side_effects=True, vmem_limit_bytes=60 * 2**20
        ),
        cost_estimate=pl.CostEstimate(
            flops=4 * tokens * 16 * features * units, bytes_accessed=4 * depth * units, transcendentals=0
        ),
        name="up_projection",
    )(activations, weight_codes, block_scales, out_grad)


def solution(mesh):
    return jax.shard_map(
        local,
        mesh=mesh,
        in_specs=(
            P(("dp", "col"), "row"),
            P("col", "row"),
            P("col", "row"),
            P(("dp", "col"), "row"),
        ),
        out_specs=(P(("dp", "col"), "row"), P(("dp", "col"), "row")),
        check_vma=False,
    )
```

```python
import jax
import jax.numpy as jnp
from jax import lax
from jax.experimental import pallas as pl
from jax.experimental.pallas import tpu as pltpu
from jax.sharding import PartitionSpec as P

QB = 128
F32 = jnp.float32
BF16 = jnp.bfloat16
MESH = pl.DeviceIdType.MESH


def kernel(
    act_hbm, codes_hbm, scales_ref, grad_hbm, proj_ref, igrad_ref,
    codes, grad, weight, acts, total,
    part, part_out, part_in_half, part_in, sums, far_out, far_in_half, far_in,
    proj_out, proj_in, igrad_out, igrad_in,
    local_sem, swap_send, swap_recv,
    wz_send, wz_recv, wy_send, wy_recv,
    az_send, az_recv, ax_send, ax_recv,
    gx_send, gx_recv, gz_send, gz_recv,
):
    dp, row, zl = lax.axis_index("dp"), lax.axis_index("row"), lax.axis_index("col")
    y, c = dp // 2, dp % 2
    zh, x = row // 4, row % 4

    def at(dy=0, dc=0, dz=0, dx=0):
        return (((y + dy) % 4) * 2 + (c + dc) % 2, ((zh + dz) % 4) * 4 + (x + dx) % 4, zl)

    LEFT, RIGHT = -1, 1
    x_at = {d: at(dx=d) for d in (LEFT, RIGHT)}
    y_at = {d: at(dy=d) for d in (LEFT, RIGHT)}
    z_at = {d: at(dz=d) for d in (LEFT, RIGHT)}
    z_cross = {d: at(dz=d, dc=1) for d in (LEFT, RIGHT)}
    other_core = at(dc=1)

    def line_at(col):
        return (dp, row, col)

    s_of = [zl, zl + 1 - 2 * (zl % 2), (zl + 2) % 4, 3 - zl]
    inside = (zl == 1) | (zl == 2)

    copies = []

    def remote(src, dst, ssem, rsem, dev):
        return pltpu.make_async_remote_copy(
            src_ref=src, dst_ref=dst, send_sem=ssem, recv_sem=rsem, device_id=dev, device_id_type=MESH
        )

    def send(src, dst, ssem, rsem, dev):
        copy = remote(src, dst, ssem, rsem, dev)
        copy.start()
        copies.append(copy)

    def arrived(dst, ssem, rsem):
        remote(dst, dst, ssem, rsem, other_core).wait_recv()

    def tile(i, size):
        return pl.ds(pl.multiple_of(i * size, size), size)

    def half_slice(s, dy, h):
        return weight.at[s, tile((y + dy) % 4 * 2 + h, QB // 2)]

    my_tokens, their_tokens = tile(c, 256), tile(1 - c, 256)

    load_codes = [
        pltpu.make_async_copy(codes_hbm.at[tile((y + i) % 4 * 2 + c, QB)], codes.at[i], local_sem.at[i]) for i in range(4)
    ]
    load_act = pltpu.make_async_copy(
        act_hbm.at[:, tile(c, QB)], acts.at[row, my_tokens], local_sem.at[4]
    )
    load_grad = pltpu.make_async_copy(grad_hbm, grad.at[my_tokens], local_sem.at[5])
    for load in (load_codes[0], load_act, load_grad, *load_codes[1:]):
        load.start()

    barrier = pltpu.get_barrier_semaphore()
    for dev in (*x_at.values(), *y_at.values(), *z_at.values(), *z_cross.values(), other_core):
        pl.semaphore_signal(barrier, inc=1, device_id=dev, device_id_type=MESH)

    @pl.when(zl > 0)
    def _():
        pl.semaphore_signal(barrier, inc=1, device_id=line_at(zl - 1), device_id_type=MESH)

    @pl.when(zl < 3)
    def _():
        pl.semaphore_signal(barrier, inc=1, device_id=line_at(zl + 1), device_id_type=MESH)

    scales = scales_ref[...].astype(F32)
    scale_row = lax.broadcasted_iota(jnp.int32, scales.shape, 0)

    def dequantize(i):
        block = (y + i) % 4
        scale = jnp.sum(jnp.where(scale_row == block * 2 + c, scales, 0.0), axis=0, keepdims=True).astype(BF16)
        load_codes[i].wait()
        for b in range(codes.shape[2] // QB):
            cols = pl.ds(b * QB, QB)
            weight[zl, tile(block, QB), cols] = codes[i, :, cols] * scale[:, b:b + 1]

    dequantize(0)
    pl.semaphore_wait(barrier, 9 + jnp.where(zl > 0, 1, 0) + jnp.where(zl < 3, 1, 0))

    their_act = act_hbm.at[:, tile(1 - c, QB)]
    send(their_act, acts.at[row, my_tokens], swap_send.at[0], swap_recv.at[0], other_core)
    send(grad_hbm, grad.at[my_tokens], swap_send.at[1], swap_recv.at[1], other_core)

    def take_act():
        load_act.wait()
        arrived(acts.at[row, their_tokens], swap_send.at[0], swap_recv.at[0])

    def take_grad():
        load_grad.wait()
        arrived(grad.at[their_tokens], swap_send.at[1], swap_recv.at[1])

    def line_copy(s, target, slot, h):
        w = half_slice(s, 0, h)
        return remote(w, w, wz_send.at[slot, h], wz_recv.at[s, h], line_at(target))

    for h in (0, 1):
        @pl.when(zl < 3)
        def _():
            line_copy(zl, zl + 1, 0, h).start()

        @pl.when(zl > 0)
        def _():
            line_copy(zl, zl - 1, 1, h).start()

    first, second = pl.ds(0, 256), pl.ds(256, 256)

    ways = ((LEFT, second, first), (RIGHT, first, second))

    def acts_piece(b, block, rows):
        return acts.at[b * 4 + block, rows]

    def acts_z_own(rest):
        for i, (d, relayed, direct) in enumerate(ways):
            piece = acts_piece(zh, x, direct if rest else relayed)
            send(piece, piece, az_send.at[4 * rest + i], az_recv.at[4 * rest + i], z_at[d])

    def acts_z_relay():
        for i, (d, relayed, _) in enumerate(ways):
            piece = acts_piece((zh - d) % 4, x, relayed)
            arrived(piece, az_send.at[i], az_recv.at[i])
            send(piece, piece, az_send.at[2 + i], az_recv.at[2 + i], z_at[d])

    def acts_z_near():
        for i, (d, _, direct) in enumerate(ways):
            arrived(acts_piece((zh - d) % 4, x, direct), az_send.at[4 + i], az_recv.at[4 + i])

    def acts_z_far():
        for i, (_, relayed, _) in enumerate(ways):
            arrived(acts_piece((zh + 2) % 4, x, relayed), az_send.at[2 + i], az_recv.at[2 + i])

    def acts_x_own(k):
        for rest in (0, 1):
            for i, (d, relayed, direct) in enumerate(ways):
                piece = acts_piece((zh + k) % 4, x, direct if rest else relayed)
                send(piece, piece, ax_send.at[k, 4 * rest + i], ax_recv.at[k, 4 * rest + i], x_at[d])

    def acts_x_relay(k):
        for i, (d, relayed, _) in enumerate(ways):
            piece = acts_piece((zh + k) % 4, (x - d) % 4, relayed)
            arrived(piece, ax_send.at[k, i], ax_recv.at[k, i])
            send(piece, piece, ax_send.at[k, 2 + i], ax_recv.at[k, 2 + i], x_at[d])

    def acts_x_far(k):
        for i, (d, relayed, direct) in enumerate(ways):
            arrived(acts_piece((zh + k) % 4, (x - d) % 4, direct), ax_send.at[k, 4 + i], ax_recv.at[k, 4 + i])
            arrived(acts_piece((zh + k) % 4, (x + 2) % 4, relayed), ax_send.at[k, 2 + i], ax_recv.at[k, 2 + i])

    def w_take(k, h):
        s = s_of[k]
        arrived(half_slice(s, 0, h), wz_send.at[0, h], wz_recv.at[s, h])
        onward = jnp.where(s > zl, zl - 1, zl + 1)

        @pl.when((onward >= 0) & (onward <= 3))
        def _():
            line_copy(s, onward, 1 + k, h).start()

    def w_take_inside(h):
        @pl.when(inside)
        def _():
            w_take(3, h)

    def w_take_end(h):
        @pl.when(jnp.logical_not(inside))
        def _():
            w_take(3, h)

    def w_y_own(k, h):
        w = half_slice(s_of[k], 0, h)
        for i, d in enumerate((LEFT, RIGHT)):
            send(w, w, wy_send.at[k, i, h], wy_recv.at[k, i, h], y_at[d])

    def w_y_relay(k):
        for i, (d, h) in enumerate(((LEFT, 1), (RIGHT, 0))):
            w = half_slice(s_of[k], -d, h)
            arrived(w, wy_send.at[k, i, h], wy_recv.at[k, i, h])
            send(w, w, wy_send.at[k, 2 + i, h], wy_recv.at[k, 2 + i, h], y_at[d])

    def w_y_rest(k):
        for i, (d, h) in enumerate(((LEFT, 0), (RIGHT, 1))):
            arrived(half_slice(s_of[k], -d, h), wy_send.at[k, i, h], wy_recv.at[k, i, h])
        for i, h in enumerate((1, 0)):
            arrived(half_slice(s_of[k], 2, h), wy_send.at[k, 2 + i, h], wy_recv.at[k, 2 + i, h])

    def span(rows):
        return slice(rows.start, rows.start + rows.size)

    def share(k, dx, rows):
        return part[k, rows, tile((x + dx) % 4, QB)]

    def g_x_first(k):
        part[k] = lax.dot_general(grad[...], weight[s_of[k]], (((1,), (1,)), ((), ())), preferred_element_type=F32)
        part_out[k, 2] = share(k, 2, slice(None)).astype(BF16)
        for i, (d, relayed, _) in enumerate(ways):
            send(part_out.at[k, 2, relayed], part_in_half.at[k, i], gx_send.at[k, i], gx_recv.at[k, i], x_at[d])
        for i, (d, _, direct) in enumerate(ways):
            part_out[k, i, direct] = share(k, d, direct).astype(BF16)
            send(part_out.at[k, i, direct], part_in.at[k, i, direct], gx_send.at[k, 4 + i], gx_recv.at[k, 4 + i], x_at[d])

    def g_x_second(k):
        for i, (d, relayed, _) in enumerate(ways):
            arrived(part_in_half.at[k, i], gx_send.at[k, i], gx_recv.at[k, i])
            part_out[k, i, relayed] = (share(k, d, relayed) + part_in_half[k, i].astype(F32)).astype(BF16)
            send(part_out.at[k, i, relayed], part_in.at[k, i, relayed], gx_send.at[k, 2 + i], gx_recv.at[k, 2 + i], x_at[d])

    def far_copy(slot):
        i = slot % 2
        d, relayed, direct = ways[i]
        if slot < 2:
            return remote(far_out.at[2, relayed], far_in_half.at[i], gz_send.at[slot], gz_recv.at[slot], z_at[d])
        rows = relayed if slot < 4 else direct
        core = rows.start // 256
        target = (((y * 2) + core), ((zh + d) % 4) * 4 + x, zl)
        return remote(far_out.at[i, rows], far_in.at[i, c], gz_send.at[slot], gz_recv.at[2 + 2 * i + c], target)

    def igrad_copy():
        return remote(igrad_out, igrad_in, swap_send.at[2], swap_recv.at[2], other_core)

    def g_x_sum(k):
        own = share(k, 0, slice(None))
        for i, (_, relayed, direct) in enumerate(ways):
            arrived(part_in.at[k, i, direct], gx_send.at[k, 4 + i], gx_recv.at[k, 4 + i])
            arrived(part_in.at[k, i, relayed], gx_send.at[k, 2 + i], gx_recv.at[k, 2 + i])
            own += part_in[k, i].astype(F32)
        away = (s_of[k] - zh) % 4

        @pl.when(away == 2)
        def _():
            far_out[2] = own.astype(BF16)
            far_copy(0).start()
            far_copy(1).start()

        for i, (d, relayed, direct) in enumerate(ways):
            @pl.when(away == d % 4)
            def _():
                far_out[i, direct] = own[span(direct)].astype(BF16)
                far_copy(4 + i).start()
                sums[1 + i] = own

        @pl.when(away == 0)
        def _():
            sums[0] = own
            igrad_out[...] = sums[0, their_tokens].astype(BF16)
            igrad_copy().start()

    def g_z_second(k):
        away = (s_of[k] - zh) % 4
        for i, (d, relayed, _) in enumerate(ways):
            @pl.when(away == d % 4)
            def _():
                arrived(far_in_half.at[i], gz_send.at[i], gz_recv.at[i])
                far_out[i, relayed] = (sums[1 + i, relayed] + far_in_half[i].astype(F32)).astype(BF16)
                far_copy(2 + i).start()

    def g_z_sum():
        arrived(igrad_in, swap_send.at[2], swap_recv.at[2])
        parts = [sums[0, my_tokens], igrad_in[...].astype(F32)]
        for j, core in enumerate((c, 1 - c)):
            for i in range(2):
                slot = 2 + 2 * i + core
                arrived(far_in.at[i, core], gz_send.at[2], gz_recv.at[slot])
                parts[j] += far_in[i, core].astype(F32)
            igrad_ref[:, tile(core, QB)] = parts[j].astype(BF16)

    def forward(k):
        s = (zh + k) % 4
        rows = jnp.concatenate([acts[s * 4 + i] for i in range(4)], axis=1)
        term = jnp.dot(rows, weight[s], preferred_element_type=F32)
        if k == 0:
            total[...] = term
        else:
            total[...] += term

    def forward_swap():
        proj_out[...] = total[their_tokens].astype(BF16)
        send(proj_out, proj_in, swap_send.at[3], swap_recv.at[3], other_core)

    def forward_sum():
        arrived(proj_in, swap_send.at[3], swap_recv.at[3])
        proj_ref[...] = (total[my_tokens] + proj_in[...].astype(F32)).astype(BF16)

    w_take_inside(1)
    w_take(1, 1)
    w_y_own(1, 1)
    take_grad()
    dequantize(2)
    dequantize(3)
    take_act()
    w_take(1, 0)
    w_y_own(1, 0)
    w_take_inside(0)
    w_take(2, 1)
    w_y_own(2, 1)
    w_take(2, 0)
    w_y_relay(1)
    w_y_own(2, 0)
    acts_x_own(0)
    acts_x_relay(0)
    dequantize(1)
    w_take_end(1)
    w_take_end(0)
    g_x_first(0)
    w_y_own(3, 0)
    acts_z_own(0)
    w_y_own(3, 1)
    w_y_rest(1)
    g_x_second(0)
    acts_z_own(1)
    w_y_relay(2)
    g_x_first(1)
    w_y_relay(3)
    g_x_second(1)
    w_y_rest(2)
    acts_z_relay()
    g_x_first(2)
    w_y_rest(3)
    g_x_first(3)
    g_x_second(2)
    g_x_sum(1)
    g_x_second(3)
    acts_z_near()
    g_x_sum(0)
    acts_z_far()
    acts_x_own(3)
    g_x_sum(2)
    acts_x_own(1)
    g_x_sum(3)
    acts_x_far(0)
    acts_x_own(2)
    acts_x_relay(1)
    forward(0)
    g_z_second(0)
    acts_x_relay(3)
    g_z_second(2)
    g_z_second(1)
    acts_x_relay(2)
    g_z_second(3)
    acts_x_far(1)
    forward(1)
    acts_x_far(3)
    forward(3)
    acts_x_far(2)
    forward(2)
    forward_swap()
    forward_sum()
    g_z_sum()

    for copy in copies:
        copy.wait_send()

    for h in (0, 1):
        @pl.when(zl < 3)
        def _():
            line_copy(zl, zl + 1, 0, h).wait_send()

        @pl.when(zl > 0)
        def _():
            line_copy(zl, zl - 1, 1, h).wait_send()

    for k in (1, 2, 3):
        onward = jnp.where(s_of[k] > zl, zl - 1, zl + 1)
        for h in (0, 1):
            @pl.when((onward >= 0) & (onward <= 3))
            def _():
                line_copy(s_of[k], onward, 1 + k, h).wait_send()

    for slot in range(6):
        far_copy(slot).wait_send()
    igrad_copy().wait_send()


def hand_on(proj_in, igrad_in, proj_ref, igrad_ref, proj, igrad, sem):
    loads = [pltpu.make_async_copy(proj_in, proj, sem.at[0]), pltpu.make_async_copy(igrad_in, igrad, sem.at[1])]
    stores = [pltpu.make_async_copy(proj, proj_ref, sem.at[2]), pltpu.make_async_copy(igrad, igrad_ref, sem.at[3])]
    for copy in loads:
        copy.start()
    for load, store in zip(loads, stores):
        load.wait()
        store.start()
    for copy in stores:
        copy.wait()


def local(activations, weight_codes, block_scales, out_grad):
    tokens, features = activations.shape
    depth, units = weight_codes.shape
    any_ref = pl.BlockSpec(memory_space=pl.ANY)
    vmem_ref = pl.BlockSpec(memory_space=pltpu.VMEM)
    dma = pltpu.SemaphoreType.DMA
    rows = depth // 2
    share = (2 * tokens, features // 2)
    half_share = (tokens, features // 2)
    results = pl.pallas_call(
        kernel,
        out_shape=(
            jax.ShapeDtypeStruct((tokens, units), BF16),
            jax.ShapeDtypeStruct((tokens, features), BF16),
        ),
        in_specs=[any_ref, any_ref, vmem_ref, any_ref],
        out_specs=(vmem_ref, vmem_ref),
        scratch_shapes=[
            pltpu.VMEM((4, QB, units), BF16),
            pltpu.VMEM((2 * tokens, units), BF16),
            pltpu.VMEM((4, rows, units), BF16),
            pltpu.VMEM((16, 2 * tokens, QB), BF16),
            pltpu.VMEM((2 * tokens, units), F32),
            pltpu.VMEM((4, 2 * tokens, rows), F32),
            pltpu.VMEM((4, 3, *share), BF16),
            pltpu.VMEM((4, 2, *half_share), BF16),
            pltpu.VMEM((4, 2, *share), BF16),
            pltpu.VMEM((3, *share), F32),
            pltpu.VMEM((3, *share), BF16),
            pltpu.VMEM((2, *half_share), BF16),
            pltpu.VMEM((2, 2, *half_share), BF16),
            pltpu.VMEM((tokens, units), BF16),
            pltpu.VMEM((tokens, units), BF16),
            pltpu.VMEM(half_share, BF16),
            pltpu.VMEM(half_share, BF16),
            dma((6,)), dma((4,)), dma((4,)),
            dma((5, 2)), dma((4, 2)),
            dma((4, 4, 2)), dma((4, 4, 2)),
            dma((6,)), dma((6,)),
            dma((4, 6)), dma((4, 6)),
            dma((4, 6)), dma((4, 6)),
            dma((6,)), dma((6,)),
        ],
        compiler_params=pltpu.CompilerParams(
            collective_id=0, has_side_effects=True, vmem_limit_bytes=60 * 2**20
        ),
        cost_estimate=pl.CostEstimate(
            flops=4 * tokens * 16 * features * units, bytes_accessed=4 * depth * units, transcendentals=0
        ),
        name="up_projection",
    )(activations, weight_codes, block_scales, out_grad)
    return pl.pallas_call(
        hand_on,
        out_shape=tuple(jax.ShapeDtypeStruct(r.shape, r.dtype) for r in results),
        in_specs=[any_ref, any_ref],
        out_specs=(any_ref, any_ref),
        scratch_shapes=[*(pltpu.VMEM(r.shape, r.dtype) for r in results), dma((4,))],
        name="hand_on",
    )(*results)


def solution(mesh):
    return jax.shard_map(
        local,
        mesh=mesh,
        in_specs=(
            P(("dp", "col"), "row"),
            P("col", "row"),
            P("col", "row"),
            P(("dp", "col"), "row"),
        ),
        out_specs=(P(("dp", "col"), "row"), P(("dp", "col"), "row")),
        check_vma=False,
    )
```

```python
import jax
import jax.numpy as jnp
from jax import lax
from jax.experimental import pallas as pl
from jax.experimental.pallas import tpu as pltpu
from jax.sharding import PartitionSpec as P

QB = 128
F32 = jnp.float32
BF16 = jnp.bfloat16
MESH = pl.DeviceIdType.MESH


def kernel(
    act_hbm, codes_hbm, scales_ref, grad_hbm, proj_ref, igrad_ref,
    codes, grad, weight, acts, total,
    part, part_out, part_in_half, part_in, sums, far_out, far_in_half, far_in,
    proj_out, proj_in, igrad_out, igrad_in,
    local_sem, swap_send, swap_recv,
    wz_send, wz_recv, wy_send, wy_recv,
    az_send, az_recv, ax_send, ax_recv,
    gx_send, gx_recv, gz_send, gz_recv,
):
    dp, row, zl = lax.axis_index("dp"), lax.axis_index("row"), lax.axis_index("col")
    y, c = dp // 2, dp % 2
    zh, x = row // 4, row % 4

    def at(dy=0, dc=0, dz=0, dx=0):
        return (((y + dy) % 4) * 2 + (c + dc) % 2, ((zh + dz) % 4) * 4 + (x + dx) % 4, zl)

    LEFT, RIGHT = -1, 1
    x_at = {d: at(dx=d) for d in (LEFT, RIGHT)}
    y_at = {d: at(dy=d) for d in (LEFT, RIGHT)}
    z_at = {d: at(dz=d) for d in (LEFT, RIGHT)}
    z_cross = {d: at(dz=d, dc=1) for d in (LEFT, RIGHT)}
    other_core = at(dc=1)

    def line_at(col):
        return (dp, row, col)

    s_of = [zl, zl + 1 - 2 * (zl % 2), (zl + 2) % 4, 3 - zl]
    inside = (zl == 1) | (zl == 2)

    copies = []

    def remote(src, dst, ssem, rsem, dev):
        return pltpu.make_async_remote_copy(
            src_ref=src, dst_ref=dst, send_sem=ssem, recv_sem=rsem, device_id=dev, device_id_type=MESH
        )

    def send(src, dst, ssem, rsem, dev):
        copy = remote(src, dst, ssem, rsem, dev)
        copy.start()
        copies.append(copy)

    def arrived(dst, ssem, rsem):
        remote(dst, dst, ssem, rsem, other_core).wait_recv()

    def tile(i, size):
        return pl.ds(pl.multiple_of(i * size, size), size)

    def half_slice(s, dy, h):
        return weight.at[s, tile((y + dy) % 4 * 2 + h, QB // 2)]

    my_tokens, their_tokens = tile(c, 256), tile(1 - c, 256)

    load_codes = [
        pltpu.make_async_copy(codes_hbm.at[tile((y + i) % 4 * 2 + c, QB)], codes.at[i], local_sem.at[i]) for i in range(4)
    ]
    load_act = pltpu.make_async_copy(
        act_hbm.at[:, tile(c, QB)], acts.at[row, my_tokens], local_sem.at[4]
    )
    load_grad = pltpu.make_async_copy(grad_hbm, grad.at[my_tokens], local_sem.at[5])
    for load in (load_codes[0], load_act, load_grad, *load_codes[1:]):
        load.start()

    barrier = pltpu.get_barrier_semaphore()
    for dev in (*x_at.values(), *y_at.values(), *z_at.values(), *z_cross.values(), other_core):
        pl.semaphore_signal(barrier, inc=1, device_id=dev, device_id_type=MESH)

    @pl.when(zl > 0)
    def _():
        pl.semaphore_signal(barrier, inc=1, device_id=line_at(zl - 1), device_id_type=MESH)

    @pl.when(zl < 3)
    def _():
        pl.semaphore_signal(barrier, inc=1, device_id=line_at(zl + 1), device_id_type=MESH)

    scales = scales_ref[...].astype(F32)
    scale_row = lax.broadcasted_iota(jnp.int32, scales.shape, 0)

    def dequantize(i):
        block = (y + i) % 4
        scale = jnp.sum(jnp.where(scale_row == block * 2 + c, scales, 0.0), axis=0, keepdims=True).astype(BF16)
        load_codes[i].wait()
        for b in range(codes.shape[2] // QB):
            cols = pl.ds(b * QB, QB)
            weight[zl, tile(block, QB), cols] = codes[i, :, cols] * scale[:, b:b + 1]

    dequantize(0)
    pl.semaphore_wait(barrier, 9 + jnp.where(zl > 0, 1, 0) + jnp.where(zl < 3, 1, 0))

    def line_copy(s, target, slot, h):
        w = half_slice(s, 0, h)
        return remote(w, w, wz_send.at[slot, h], wz_recv.at[s, h], line_at(target))

    for h in (0, 1):
        @pl.when(zl < 3)
        def _():
            line_copy(zl, zl + 1, 0, h).start()

        @pl.when(zl > 0)
        def _():
            line_copy(zl, zl - 1, 1, h).start()

    their_act = act_hbm.at[:, tile(1 - c, QB)]
    send(their_act, acts.at[row, my_tokens], swap_send.at[0], swap_recv.at[0], other_core)
    send(grad_hbm, grad.at[my_tokens], swap_send.at[1], swap_recv.at[1], other_core)

    def take_act():
        load_act.wait()
        arrived(acts.at[row, their_tokens], swap_send.at[0], swap_recv.at[0])

    def take_grad():
        load_grad.wait()
        arrived(grad.at[their_tokens], swap_send.at[1], swap_recv.at[1])

    first, second = pl.ds(0, 256), pl.ds(256, 256)

    ways = ((LEFT, second, first), (RIGHT, first, second))

    def acts_piece(b, block, rows):
        return acts.at[b * 4 + block, rows]

    def acts_z_own(rest):
        for i, (d, relayed, direct) in enumerate(ways):
            piece = acts_piece(zh, x, direct if rest else relayed)
            send(piece, piece, az_send.at[4 * rest + i], az_recv.at[4 * rest + i], z_at[d])

    def acts_z_relay():
        for i, (d, relayed, _) in enumerate(ways):
            piece = acts_piece((zh - d) % 4, x, relayed)
            arrived(piece, az_send.at[i], az_recv.at[i])
            send(piece, piece, az_send.at[2 + i], az_recv.at[2 + i], z_at[d])

    def acts_z_near():
        for i, (d, _, direct) in enumerate(ways):
            arrived(acts_piece((zh - d) % 4, x, direct), az_send.at[4 + i], az_recv.at[4 + i])

    def acts_z_far():
        for i, (_, relayed, _) in enumerate(ways):
            arrived(acts_piece((zh + 2) % 4, x, relayed), az_send.at[2 + i], az_recv.at[2 + i])

    def acts_x_own(k):
        for rest in (0, 1):
            for i, (d, relayed, direct) in enumerate(ways):
                piece = acts_piece((zh + k) % 4, x, direct if rest else relayed)
                send(piece, piece, ax_send.at[k, 4 * rest + i], ax_recv.at[k, 4 * rest + i], x_at[d])

    def acts_x_relay(k):
        for i, (d, relayed, _) in enumerate(ways):
            piece = acts_piece((zh + k) % 4, (x - d) % 4, relayed)
            arrived(piece, ax_send.at[k, i], ax_recv.at[k, i])
            send(piece, piece, ax_send.at[k, 2 + i], ax_recv.at[k, 2 + i], x_at[d])

    def acts_x_far(k):
        for i, (d, relayed, direct) in enumerate(ways):
            arrived(acts_piece((zh + k) % 4, (x - d) % 4, direct), ax_send.at[k, 4 + i], ax_recv.at[k, 4 + i])
            arrived(acts_piece((zh + k) % 4, (x + 2) % 4, relayed), ax_send.at[k, 2 + i], ax_recv.at[k, 2 + i])

    def w_take(k, h):
        s = s_of[k]
        arrived(half_slice(s, 0, h), wz_send.at[0, h], wz_recv.at[s, h])
        onward = jnp.where(s > zl, zl - 1, zl + 1)

        @pl.when((onward >= 0) & (onward <= 3))
        def _():
            line_copy(s, onward, 1 + k, h).start()

    def w_take_inside(h):
        @pl.when(inside)
        def _():
            w_take(3, h)

    def w_take_end(h):
        @pl.when(jnp.logical_not(inside))
        def _():
            w_take(3, h)

    def w_y_own(k, h):
        w = half_slice(s_of[k], 0, h)
        for i, d in enumerate((LEFT, RIGHT)):
            send(w, w, wy_send.at[k, i, h], wy_recv.at[k, i, h], y_at[d])

    def w_y_relay(k):
        for i, (d, h) in enumerate(((LEFT, 1), (RIGHT, 0))):
            w = half_slice(s_of[k], -d, h)
            arrived(w, wy_send.at[k, i, h], wy_recv.at[k, i, h])
            send(w, w, wy_send.at[k, 2 + i, h], wy_recv.at[k, 2 + i, h], y_at[d])

    def w_y_rest(k):
        for i, (d, h) in enumerate(((LEFT, 0), (RIGHT, 1))):
            arrived(half_slice(s_of[k], -d, h), wy_send.at[k, i, h], wy_recv.at[k, i, h])
        for i, h in enumerate((1, 0)):
            arrived(half_slice(s_of[k], 2, h), wy_send.at[k, 2 + i, h], wy_recv.at[k, 2 + i, h])

    def span(rows):
        return slice(rows.start, rows.start + rows.size)

    def share(k, dx, rows):
        return part[k, rows, tile((x + dx) % 4, QB)]

    def g_x_first(k):
        part[k] = lax.dot_general(grad[...], weight[s_of[k]], (((1,), (1,)), ((), ())), preferred_element_type=F32)
        part_out[k, 2] = share(k, 2, slice(None)).astype(BF16)
        for i, (d, relayed, _) in enumerate(ways):
            send(part_out.at[k, 2, relayed], part_in_half.at[k, i], gx_send.at[k, i], gx_recv.at[k, i], x_at[d])
        for i, (d, _, direct) in enumerate(ways):
            part_out[k, i, direct] = share(k, d, direct).astype(BF16)
            send(part_out.at[k, i, direct], part_in.at[k, i, direct], gx_send.at[k, 4 + i], gx_recv.at[k, 4 + i], x_at[d])

    def g_x_second(k):
        for i, (d, relayed, _) in enumerate(ways):
            arrived(part_in_half.at[k, i], gx_send.at[k, i], gx_recv.at[k, i])
            part_out[k, i, relayed] = (share(k, d, relayed) + part_in_half[k, i].astype(F32)).astype(BF16)
            send(part_out.at[k, i, relayed], part_in.at[k, i, relayed], gx_send.at[k, 2 + i], gx_recv.at[k, 2 + i], x_at[d])

    def far_copy(slot):
        i = slot % 2
        d, relayed, direct = ways[i]
        if slot < 2:
            return remote(far_out.at[2, relayed], far_in_half.at[i], gz_send.at[slot], gz_recv.at[slot], z_at[d])
        rows = relayed if slot < 4 else direct
        core = rows.start // 256
        target = (((y * 2) + core), ((zh + d) % 4) * 4 + x, zl)
        return remote(far_out.at[i, rows], far_in.at[i, c], gz_send.at[slot], gz_recv.at[2 + 2 * i + c], target)

    def igrad_copy():
        return remote(igrad_out, igrad_in, swap_send.at[2], swap_recv.at[2], other_core)

    def g_x_sum(k):
        own = share(k, 0, slice(None))
        for i, (_, relayed, direct) in enumerate(ways):
            arrived(part_in.at[k, i, direct], gx_send.at[k, 4 + i], gx_recv.at[k, 4 + i])
            arrived(part_in.at[k, i, relayed], gx_send.at[k, 2 + i], gx_recv.at[k, 2 + i])
            own += part_in[k, i].astype(F32)
        away = (s_of[k] - zh) % 4

        @pl.when(away == 2)
        def _():
            far_out[2] = own.astype(BF16)
            far_copy(0).start()
            far_copy(1).start()

        for i, (d, relayed, direct) in enumerate(ways):
            @pl.when(away == d % 4)
            def _():
                far_out[i, direct] = own[span(direct)].astype(BF16)
                far_copy(4 + i).start()
                sums[1 + i] = own

        @pl.when(away == 0)
        def _():
            sums[0] = own
            igrad_out[...] = sums[0, their_tokens].astype(BF16)
            igrad_copy().start()

    def g_z_second(k):
        away = (s_of[k] - zh) % 4
        for i, (d, relayed, _) in enumerate(ways):
            @pl.when(away == d % 4)
            def _():
                arrived(far_in_half.at[i], gz_send.at[i], gz_recv.at[i])
                far_out[i, relayed] = (sums[1 + i, relayed] + far_in_half[i].astype(F32)).astype(BF16)
                far_copy(2 + i).start()

    def g_z_sum():
        arrived(igrad_in, swap_send.at[2], swap_recv.at[2])
        parts = [sums[0, my_tokens], igrad_in[...].astype(F32)]
        for j, core in enumerate((c, 1 - c)):
            for i in range(2):
                slot = 2 + 2 * i + core
                arrived(far_in.at[i, core], gz_send.at[2], gz_recv.at[slot])
                parts[j] += far_in[i, core].astype(F32)
            igrad_ref[:, tile(core, QB)] = parts[j].astype(BF16)

    def forward(k):
        s = (zh + k) % 4
        rows = jnp.concatenate([acts[s * 4 + i] for i in range(4)], axis=1)
        term = jnp.dot(rows, weight[s], preferred_element_type=F32)
        if k == 0:
            total[...] = term
        else:
            total[...] += term

    def forward_swap():
        proj_out[...] = total[their_tokens].astype(BF16)
        send(proj_out, proj_in, swap_send.at[3], swap_recv.at[3], other_core)

    def forward_sum():
        arrived(proj_in, swap_send.at[3], swap_recv.at[3])
        proj_ref[...] = (total[my_tokens] + proj_in[...].astype(F32)).astype(BF16)

    w_take_inside(0)
    w_take(1, 0)
    w_y_own(1, 0)
    take_grad()
    dequantize(2)
    dequantize(3)
    take_act()
    w_take(1, 1)
    w_y_own(1, 1)
    w_take_inside(1)
    w_take(2, 0)
    w_y_own(2, 0)
    w_take(2, 1)
    w_y_relay(1)
    w_y_own(2, 1)
    acts_x_own(0)
    acts_x_relay(0)
    dequantize(1)
    w_take_end(0)
    w_take_end(1)
    g_x_first(0)
    w_y_own(3, 0)
    acts_z_own(0)
    w_y_own(3, 1)
    w_y_rest(1)
    g_x_second(0)
    acts_z_own(1)
    w_y_relay(2)
    g_x_first(1)
    w_y_relay(3)
    g_x_second(1)
    w_y_rest(2)
    acts_z_relay()
    g_x_first(2)
    w_y_rest(3)
    g_x_first(3)
    g_x_second(2)
    g_x_sum(1)
    g_x_second(3)
    acts_z_near()
    g_x_sum(0)
    acts_z_far()
    acts_x_own(3)
    g_x_sum(2)
    acts_x_own(1)
    g_x_sum(3)
    acts_x_far(0)
    acts_x_own(2)
    acts_x_relay(1)
    forward(0)
    g_z_second(0)
    acts_x_relay(3)
    g_z_second(2)
    g_z_second(1)
    acts_x_relay(2)
    g_z_second(3)
    acts_x_far(1)
    forward(1)
    acts_x_far(3)
    forward(3)
    acts_x_far(2)
    forward(2)
    forward_swap()
    forward_sum()
    g_z_sum()


    for copy in copies:
        copy.wait_send()

    for h in (0, 1):
        @pl.when(zl < 3)
        def _():
            line_copy(zl, zl + 1, 0, h).wait_send()

        @pl.when(zl > 0)
        def _():
            line_copy(zl, zl - 1, 1, h).wait_send()

    for k in (1, 2, 3):
        onward = jnp.where(s_of[k] > zl, zl - 1, zl + 1)
        for h in (0, 1):
            @pl.when((onward >= 0) & (onward <= 3))
            def _():
                line_copy(s_of[k], onward, 1 + k, h).wait_send()

    for slot in range(6):
        far_copy(slot).wait_send()
    igrad_copy().wait_send()


def hand_on(proj_in, igrad_in, proj_ref, igrad_ref, proj, igrad, sem):
    loads = [pltpu.make_async_copy(proj_in, proj, sem.at[0]), pltpu.make_async_copy(igrad_in, igrad, sem.at[1])]
    stores = [pltpu.make_async_copy(proj, proj_ref, sem.at[2]), pltpu.make_async_copy(igrad, igrad_ref, sem.at[3])]
    for copy in loads:
        copy.start()
    for load, store in zip(loads, stores):
        load.wait()
        store.start()
    for copy in stores:
        copy.wait()


def local(activations, weight_codes, block_scales, out_grad):
    tokens, features = activations.shape
    depth, units = weight_codes.shape
    any_ref = pl.BlockSpec(memory_space=pl.ANY)
    vmem_ref = pl.BlockSpec(memory_space=pltpu.VMEM)
    dma = pltpu.SemaphoreType.DMA
    rows = depth // 2
    share = (2 * tokens, features // 2)
    half_share = (tokens, features // 2)
    results = pl.pallas_call(
        kernel,
        out_shape=(
            jax.ShapeDtypeStruct((tokens, units), BF16),
            jax.ShapeDtypeStruct((tokens, features), BF16),
        ),
        in_specs=[any_ref, any_ref, vmem_ref, any_ref],
        out_specs=(vmem_ref, vmem_ref),
        scratch_shapes=[
            pltpu.VMEM((4, QB, units), BF16),
            pltpu.VMEM((2 * tokens, units), BF16),
            pltpu.VMEM((4, rows, units), BF16),
            pltpu.VMEM((16, 2 * tokens, QB), BF16),
            pltpu.VMEM((2 * tokens, units), F32),
            pltpu.VMEM((4, 2 * tokens, rows), F32),
            pltpu.VMEM((4, 3, *share), BF16),
            pltpu.VMEM((4, 2, *half_share), BF16),
            pltpu.VMEM((4, 2, *share), BF16),
            pltpu.VMEM((3, *share), F32),
            pltpu.VMEM((3, *share), BF16),
            pltpu.VMEM((2, *half_share), BF16),
            pltpu.VMEM((2, 2, *half_share), BF16),
            pltpu.VMEM((tokens, units), BF16),
            pltpu.VMEM((tokens, units), BF16),
            pltpu.VMEM(half_share, BF16),
            pltpu.VMEM(half_share, BF16),
            dma((6,)), dma((4,)), dma((4,)),
            dma((5, 2)), dma((4, 2)),
            dma((4, 4, 2)), dma((4, 4, 2)),
            dma((6,)), dma((6,)),
            dma((4, 6)), dma((4, 6)),
            dma((4, 6)), dma((4, 6)),
            dma((6,)), dma((6,)),
        ],
        compiler_params=pltpu.CompilerParams(
            collective_id=0, has_side_effects=True, vmem_limit_bytes=60 * 2**20
        ),
        cost_estimate=pl.CostEstimate(
            flops=4 * tokens * 16 * features * units, bytes_accessed=4 * depth * units, transcendentals=0
        ),
        name="up_projection",
    )(activations, weight_codes, block_scales, out_grad)
    return pl.pallas_call(
        hand_on,
        out_shape=tuple(jax.ShapeDtypeStruct(r.shape, r.dtype) for r in results),
        in_specs=[any_ref, any_ref],
        out_specs=(any_ref, any_ref),
        scratch_shapes=[*(pltpu.VMEM(r.shape, r.dtype) for r in results), dma((4,))],
        name="hand_on",
    )(*results)


def solution(mesh):
    return jax.shard_map(
        local,
        mesh=mesh,
        in_specs=(
            P(("dp", "col"), "row"),
            P("col", "row"),
            P("col", "row"),
            P(("dp", "col"), "row"),
        ),
        out_specs=(P(("dp", "col"), "row"), P(("dp", "col"), "row")),
        check_vma=False,
    )
```
